256 devices in a mesh: design: 16 (over z_hi, y, core), space: 16 (over z_lo, x).
Axes of the slice: x: 4, y: 4, z: 8 (z_hi: 2, z_lo: 4; z = z_hi * 4 + z_lo), core: 2. Of those that a mesh axis runs over, the one named last changes fastest.
Arguments:
- initial_density: float32 [64, 256, 128], P(None, 'space'), may hold values from 0.45 to 0.75
- initial_thermal: float32 [64, 256, 128], P(None, 'space'), may hold values from 0.7 to 1.1
- boundary_mask: int32 [64, 256, 128], P(None, 'space'), may hold values 0 or 1
- samples_a: float32 [4, 14], replicated, may hold values from 0 to 1
- samples_b: float32 [4, 14], replicated, may hold values from 0 to 1
- design_index: int32 [14], replicated, may hold values from 0 to 13, each once
Outputs:
- first_order: float32 [14, 64, 256, 128], P(None, 'design', 'space')
- total_order: float32 [14, 64, 256, 128], P(None, 'design', 'space')
- variance_map: float32 [64, 256, 128], P('design', 'space')
The draws below stay inside these ranges and needn't reach their ends.
Inputs may be any that keep to these rules, and one draw needn't show every extreme that they name: `design_index`: each parameter appears exactly once.
All inputs are finite; a program needn't handle non-finite values. No bound on the sum of `boundary_mask` on one device may be relied on, other than what follows from the above.
Results may differ from the reference program's by a relative error of at most 0.0003.
Values sent between devices are 32-bit elements; how exact they have to be, the bound alone decides.
A program may use at most 64 MiB of HBM per device.

```python
import jax
import jax.numpy as jnp
from jax import lax

P_SIZE = 14
SAMPLES = 4
STEPS = 8
NY = 128
NZ = 64
GROUPS = 16
NX = 256


def set_ends(result, key, low, high):
    spot = [jax.random.randint(jax.random.fold_in(key, axis), (), 0, length) for axis, length in enumerate(result.shape)]
    main_axis = result.shape.index(max(result.shape))
    neighbour = spot[:main_axis] + [(spot[main_axis] + 1) % result.shape[main_axis]] + spot[main_axis + 1:]
    return result.at[tuple(spot)].set(low).at[tuple(neighbour)].set(high)


def level_of(stream_key, dims, cuts, low, largest):
    gain, own = 1.0, jax.random.fold_in(stream_key, 6)
    for dim, parts in cuts:
        heights = jnp.exp(jax.random.uniform(jax.random.fold_in(own, dim), (parts,), jnp.float32, low / len(cuts), largest / len(cuts)))
        gain = gain * jnp.repeat(heights, dims[dim] // parts).reshape([-1 if axis == dim else 1 for axis in range(len(dims))])
    return gain


def setup_inputs(seed: int = 0) -> dict:
    arg_keys = jax.random.split(jax.random.key(seed), 7)
    initial_density = jnp.clip(0.45 + 0.3 * jax.random.uniform(arg_keys[0], (NZ, NX, NY), jnp.float32) ** level_of(arg_keys[0], (NZ, NX, NY), ((1, 16),), -0.2, 0.2), 0.45, 0.75)
    initial_thermal = jnp.clip(0.7 + 0.40000004 * jax.random.uniform(arg_keys[1], (NZ, NX, NY), jnp.float32) ** level_of(arg_keys[1], (NZ, NX, NY), ((1, 16),), -0.2, 0.2), 0.7, 1.1)
    boundary_mask = set_ends((jax.random.randint(arg_keys[2], (NZ, NX, NY), 0, 4) < 1).astype(jnp.int32), jax.random.fold_in(arg_keys[2], 1), 0, 1)
    samples_a = jnp.clip(jax.random.uniform(arg_keys[3], (SAMPLES, P_SIZE), jnp.float32, 0.0, 1.0), 0.0, 1.0)
    samples_b = jnp.clip(jax.random.uniform(arg_keys[4], (SAMPLES, P_SIZE), jnp.float32, 0.0, 1.0), 0.0, 1.0)
    design_index = jax.random.permutation(arg_keys[5], P_SIZE).astype(jnp.int32)
    return {"initial_density": initial_density, "initial_thermal": initial_thermal, "boundary_mask": boundary_mask, "samples_a": samples_a, "samples_b": samples_b, "design_index": design_index}


def group_params(samples_a, samples_b, design_index):
    group_ids = jnp.arange(GROUPS, dtype=jnp.int32)[:, None]
    param_ids = jnp.arange(P_SIZE, dtype=jnp.int32)[None, :]
    picked = design_index[jnp.clip(group_ids - 2, 0, P_SIZE - 1)]
    take_b = (group_ids == 1) | ((group_ids >= 2) & (picked == param_ids))
    return jnp.where(take_b[:, None, :], samples_b[None], samples_a[None])


def coefficients(params):
    column = [params[:, index_k][:, None, None, None] for index_k in range(P_SIZE)]
    return (0.04 + 0.06 * column[0], 0.5 + 0.5 * column[1], 0.02 + 0.04 * column[2],
            1.0 + 3.0 * column[3], column[4], 0.2 + 0.6 * column[5], 1.0 + 0.4 * column[6],
            0.05 + 0.15 * column[7], 0.02 + 0.04 * column[8], 0.02 * column[9],
            0.5 + 0.5 * column[10], 0.5 + 0.5 * column[11], column[12], 0.3 * (column[13] - 0.5))


def ambient_at(coeffs, section_no):
    return coeffs[6] + coeffs[8] * section_no


def z_extend(field):
    return jnp.concatenate([field[:, :1], field, field[:, -1:]], 1)


def advance(density, padded, masked, coeffs, section_no):
    k_zero, k_one, pre_a, sens_b, expo_m, heat_q, amb_base, coef_h, ramp_r, source, weight_x, weight_z, growth, offset = coeffs
    centre = padded[:, 1:-1, 1:-1]
    y_plus = jnp.concatenate([centre[..., 1:], centre[..., -1:]], -1)
    y_minus = jnp.concatenate([centre[..., :1], centre[..., :-1]], -1)
    laplace = weight_x * (padded[:, 1:-1, 2:] + padded[:, 1:-1, :-2] - 2.0 * centre)
    laplace = laplace + weight_z * (padded[:, 2:, 1:-1] + padded[:, :-2, 1:-1] - 2.0 * centre)
    laplace = laplace + (y_plus + y_minus - 2.0 * centre)
    conduct = k_zero * (0.5 + k_one * density)
    densify = pre_a * jnp.exp(sens_b * (centre - 1.0) + expo_m * jnp.log(1.0 - density) - growth * section_no / STEPS)
    new_density = 1.0 - (1.0 - density) * jnp.exp(-densify)
    ambient = ambient_at(coeffs, section_no)
    new_thermal = centre + conduct * laplace + coef_h * masked * (ambient - centre) + heat_q * (new_density - density) + source * density
    return new_density, new_thermal


def evolve(params, initial_density, initial_thermal, masked):
    coeffs = coefficients(params)
    density = jnp.broadcast_to(initial_density, (params.shape[0],) + initial_density.shape)
    thermal = initial_thermal[None] + coeffs[13]
    for section_no in range(STEPS):
        ambient = jnp.broadcast_to(ambient_at(coeffs, section_no), thermal[:, :, :1].shape)
        padded = z_extend(jnp.concatenate([ambient, thermal, ambient], 2))
        density, thermal = advance(density, padded, masked, coeffs, section_no)
    return 10.0 * density


def reference(initial_density, initial_thermal, boundary_mask, samples_a, samples_b, design_index):
    masked = boundary_mask.astype(jnp.float32)
    params = group_params(samples_a, samples_b, design_index)
    resp_a = evolve(params[0], initial_density, initial_thermal, masked)
    resp_b = evolve(params[1], initial_density, initial_thermal, masked)
    pooled = jnp.concatenate([resp_a, resp_b], 0)
    average = jnp.mean(pooled, 0)
    variance = jnp.mean((pooled - average[None]) ** 2, 0)

    def mixed_terms(mixed_params):
        response = evolve(mixed_params, initial_density, initial_thermal, masked)
        first_map = variance - 0.5 * jnp.mean((resp_b - response) ** 2, 0)
        total_map = 0.5 * jnp.mean((resp_a - response) ** 2, 0)
        return first_map, total_map

    first_map, total_map = lax.map(mixed_terms, params[2:])
    return first_map, total_map, variance
```

```python
import jax
import jax.numpy as jnp
import numpy as np
from jax import lax
from jax.experimental import pallas as pl
from jax.experimental.pallas import tpu as pltpu
from jax.sharding import PartitionSpec as P

P_SIZE = 14
SAMPLES = 4
STEPS = 8
GROUPS = 16

HALO = 7
XS = 16
LAYERS = XS + 2 * HALO
ROWS = 40
PEERS = 8
MINE = 8
BLOCK = 4
LOG2E = float(np.log2(np.e))
MESH = pl.DeviceIdType.MESH


def splat(value):
    return jnp.full((8, 128), value, jnp.float32)


def sample_coefficients(sa, sb, di, group, sample):
    picked = di[jnp.maximum(group - 2, 0)]
    t = []
    for p in range(P_SIZE):
        take_b = (group == 1) | ((group >= 2) & (picked == p))
        t.append(splat(jnp.where(take_b, sb[sample, p], sa[sample, p])))
    k0 = 0.04 + 0.06 * t[0]
    k1 = 0.5 + 0.5 * t[1]
    a = 0.02 + 0.04 * t[2]
    b2 = LOG2E * (1.0 + 3.0 * t[3])
    m = t[4]
    q = 0.2 + 0.6 * t[5]
    amb = 1.0 + 0.4 * t[6]
    h = 0.05 + 0.15 * t[7]
    ramp = 0.02 + 0.04 * t[8]
    src = 0.02 * t[9]
    wx = 0.5 + 0.5 * t[10]
    wz = 0.5 + 0.5 * t[11]
    gr = t[12]
    off = 0.3 * (t[13] - 0.5)
    c1 = k0 * k1
    inv = 1.0 / c1
    c0 = k0 * (0.5 + k1)
    lc1 = LOG2E * jnp.log(c1)
    first = LOG2E * jnp.log(a * LOG2E) + b2 * (amb - 1.0) - m * lc1
    return dict(
        wx=wx,
        wz=wz,
        wc=2.0 * (wx + wz + 1.0),
        p=b2 * (q - src) * inv,
        r=b2 * q * inv,
        k=b2 * (src * (1.0 - c0 * inv) - ramp),
        c0=c0,
        c1=c1,
        m=m,
        h=h,
        lc1=lc1,
        b2=b2,
        start=b2 * (off - amb),
        arg=first,
        arg_step=b2 * ramp - gr * (LOG2E / STEPS),
        out=10.0 * inv,
    )


def kernel(
    dens_ref,
    temp_ref,
    mask_ref,
    sa,
    sb,
    di,
    first_ref,
    total_ref,
    var_ref,
    t0,
    d0,
    m0,
    v0,
    u0,
    theta_a,
    theta_b,
    u_ref,
    w_ref,
    h_ref,
    rsp,
    recv,
    halo_send,
    halo_recv,
    send_sem,
    recv_sem,
):
    d_index = lax.axis_index("design")
    s_index = lax.axis_index("space")
    s_count = lax.axis_size("space")
    zh = d_index // PEERS
    loc = d_index % PEERS
    right = (s_index + 1) % s_count
    left = (s_index + s_count - 1) % s_count

    def peer(j):
        return (loc + j) % PEERS

    barrier = pltpu.get_barrier_semaphore()
    for side in (left, right):
        pl.semaphore_signal(barrier, inc=1, device_id=(d_index, side), device_id_type=MESH)
    for j in range(1, PEERS):
        pl.semaphore_signal(
            barrier, inc=1, device_id=(zh * PEERS + peer(j), s_index), device_id_type=MESH
        )

    def stage(x, carry):
        for k in range(ROWS // 8):
            rows = pl.ds((24 * zh + 8 * k) * XS + x, 8, stride=XS)
            at = (HALO + x, pl.ds(8 * k, 8))
            t0[at] = temp_ref[rows, :]
            d0[at] = dens_ref[rows, :]
            m0[at] = mask_ref[rows, :].astype(jnp.float32)
        return carry

    lax.fori_loop(0, XS, stage, 0)
    pl.semaphore_wait(barrier, PEERS + 1)

    halo = []
    for index, (ref, width) in enumerate(((t0, HALO), (d0, HALO - 1), (m0, HALO - 1))):
        for way, (source, target, side) in enumerate(
            ((HALO, HALO + XS, left), (HALO + XS - width, HALO - width, right))
        ):
            copy = pltpu.make_async_remote_copy(
                src_ref=ref.at[pl.ds(source, width)],
                dst_ref=ref.at[pl.ds(target, width)],
                send_sem=halo_send.at[2 * index + way],
                recv_sem=halo_recv.at[2 * index + way],
                device_id=(d_index, side),
                device_id_type=MESH,
            )
            copy.start()
            halo.append(copy)
    for copy in halo:
        copy.wait()

    def prepare(l, carry):
        for k in range(ROWS // 8):
            at = (l, pl.ds(8 * k, 8))
            v = 1.0 - d0[at]
            v0[at] = v
            u0[at] = LOG2E * jnp.log(v)
        return carry

    lax.fori_loop(1, LAYERS - 1, prepare, 0)

    lane = lax.broadcasted_iota(jnp.int32, (8, 128), 1)
    row = lax.broadcasted_iota(jnp.int32, (8, 128), 0)
    lane_first, lane_last = lane == 0, lane == 127
    row_first, row_last = row == 0, row == 7
    zero = jnp.zeros((8, 128), jnp.float32)

    def evolve(i, carry):
        c = sample_coefficients(sa, sb, di, 2 * loc + i // SAMPLES, i % SAMPLES)

        def begin(l, carry):
            for k in range(ROWS // 8):
                theta_a[l, pl.ds(8 + 8 * k, 8)] = c["b2"] * t0[l, pl.ds(8 * k, 8)] + c["start"]
            return carry

        lax.fori_loop(0, LAYERS, begin, 0)

        def edges(ref):
            @pl.when(s_index == 0)
            def _():
                for k in range(ROWS // 8):
                    ref[HALO - 1, pl.ds(8 + 8 * k, 8)] = zero

            @pl.when(s_index == s_count - 1)
            def _():
                for k in range(ROWS // 8):
                    ref[HALO + XS, pl.ds(8 + 8 * k, 8)] = zero

        edges(theta_a)
        for n in range(STEPS - 1):
            src, dst = (theta_a, theta_b) if n % 2 == 0 else (theta_b, theta_a)
            low = 1 + 2 * (n // 2)
            arg = c["arg"] + float(n) * c["arg_step"]
            arg0 = arg + c["m"] * c["lc1"]
            last = n == STEPS - 2
            tiles = 4 if last else ROWS // 8

            def block(b, carry, n=n, src=src, dst=dst, low=low, arg=arg, arg0=arg0, last=last, tiles=tiles):
                base = low + BLOCK * b
                for k in range(tiles):
                    z = pl.multiple_of(8 * zh, 8) + 8 * k if last else 8 * k
                    column = [src[base - 1 + j, pl.ds(8 + z, 8)] for j in range(BLOCK + 2)]
                    for j in range(BLOCK):
                        l = base + j
                        at = (l, pl.ds(z, 8))
                        mid = column[j + 1]
                        z_minus = src[l, pl.ds(7 + z, 8)]
                        z_plus = src[l, pl.ds(9 + z, 8)]
                        if k == 0:
                            z_minus = jnp.where(row_first & (zh == 0) if last else row_first, mid, z_minus)
                        if k == tiles - 1:
                            z_plus = jnp.where(row_last & (zh == 1) if last else row_last, mid, z_plus)
                        y_minus = jnp.where(lane_first, mid, pltpu.roll(mid, 1, 1))
                        y_plus = jnp.where(lane_last, mid, pltpu.roll(mid, 127, 1))
                        laplace = (
                            c["wx"] * (column[j] + column[j + 2])
                            + c["wz"] * (z_minus + z_plus)
                            + ((y_minus + y_plus) - (c["wc"] * mid + c["p"]))
                        )
                        if n == 0:
                            v, u = v0[at], u0[at]
                            conduct = c["c0"] - c["c1"] * v
                            grow = jnp.exp2(mid + (c["m"] * u + arg0))
                            new_u = (u + c["lc1"]) - grow
                            keep = 1.0 - c["h"] * m0[at]
                            h_ref[at] = keep
                        else:
                            u, conduct, keep = u_ref[at], w_ref[at], h_ref[at]
                            new_u = u - jnp.exp2(mid + (c["m"] * u + arg))
                        new_conduct = c["c0"] - jnp.exp2(new_u)
                        u_ref[at] = new_u
                        if not last:
                            w_ref[at] = new_conduct
                        dst[l, pl.ds(8 + z, 8)] = (
                            keep * mid + conduct * laplace + (c["r"] * new_conduct + c["k"])
                        )
                return carry

            lax.fori_loop(0, (LAYERS - 2 - 4 * (n // 2)) // BLOCK, block, 0)
            if not last:
                edges(dst)

        src = theta_a if (STEPS - 1) % 2 == 0 else theta_b
        arg = c["arg"] + float(STEPS - 1) * c["arg_step"]

        def finish(x, carry):
            l = HALO + x
            for k in range(4):
                z = pl.multiple_of(8 * zh, 8) + 8 * k
                u = u_ref[l, pl.ds(z, 8)]
                new_u = u - jnp.exp2(src[l, pl.ds(8 + z, 8)] + (c["m"] * u + arg))
                rsp[i, pl.ds(8 * k * XS + x, 8, stride=XS), :] = 10.0 - c["out"] * jnp.exp2(new_u)
            return carry

        lax.fori_loop(0, XS, finish, 0)
        for j in range(1, PEERS):
            sends(i, j).start()
        own = pl.ds(pl.multiple_of(64 * loc, 8), 64)
        recv[loc * MINE + i] = rsp[i, own, :]
        return carry

    def sends(i, j):
        return pltpu.make_async_remote_copy(
            src_ref=rsp.at[i, pl.ds(pl.multiple_of(64 * peer(j), 8), 64)],
            dst_ref=recv.at[loc * MINE + i],
            send_sem=send_sem.at[i, j - 1],
            recv_sem=recv_sem.at[i, j - 1],
            device_id=(zh * PEERS + peer(j), s_index),
            device_id_type=MESH,
        )

    lax.fori_loop(0, MINE, evolve, 0)

    def drain(i, carry):
        for j in range(1, PEERS):
            sends(i, j).wait()
        return carry

    lax.fori_loop(0, MINE, drain, 0)

    def maps(tile, carry):
        at = pl.ds(pl.multiple_of(8 * tile, 8), 8)
        resp_a = [recv[s, at, :] for s in range(SAMPLES)]
        resp_b = [recv[SAMPLES + s, at, :] for s in range(SAMPLES)]
        pooled = resp_a + resp_b
        average = sum(pooled[1:], pooled[0]) * (1.0 / len(pooled))
        spread = [(r - average) * (r - average) for r in pooled]
        variance = sum(spread[1:], spread[0]) * (1.0 / len(pooled))
        var_ref[at, :] = variance
        for g in range(GROUPS - 2):
            first = total = None
            for s in range(SAMPLES):
                mixed = recv[(g + 2) * SAMPLES + s, at, :]
                to_b, to_a = resp_b[s] - mixed, resp_a[s] - mixed
                first = to_b * to_b if first is None else first + to_b * to_b
                total = to_a * to_a if total is None else total + to_a * to_a
            first_ref[g, at, :] = variance - (0.5 / SAMPLES) * first
            total_ref[g, at, :] = (0.5 / SAMPLES) * total
        return carry

    lax.fori_loop(0, 8, maps, 0)


def local(initial_density, initial_thermal, boundary_mask, samples_a, samples_b, design_index):
    vmem = pl.BlockSpec(memory_space=pltpu.VMEM)
    smem = pl.BlockSpec(memory_space=pltpu.SMEM)
    state = pltpu.VMEM((LAYERS, ROWS, 128), jnp.float32)
    theta = pltpu.VMEM((LAYERS, ROWS + 16, 128), jnp.float32)
    responses = pltpu.VMEM((MINE, 512, 128), jnp.float32)
    dma = pltpu.SemaphoreType.DMA
    first, total, variance = pl.pallas_call(
        kernel,
        out_shape=(
            jax.ShapeDtypeStruct((GROUPS - 2, 64, 128), jnp.float32),
            jax.ShapeDtypeStruct((GROUPS - 2, 64, 128), jnp.float32),
            jax.ShapeDtypeStruct((64, 128), jnp.float32),
        ),
        in_specs=[vmem] * 3 + [smem] * 3,
        out_specs=(vmem, vmem, vmem),
        scratch_shapes=[
            state,
            state,
            state,
            state,
            state,
            theta,
            theta,
            state,
            state,
            state,
            responses,
            pltpu.VMEM((GROUPS * SAMPLES, 64, 128), jnp.float32),
            dma((6,)),
            dma((6,)),
            dma((MINE, PEERS - 1)),
            dma((MINE, PEERS - 1)),
        ],
        compiler_params=pltpu.CompilerParams(
            collective_id=0, has_side_effects=True, vmem_limit_bytes=32 * 1024 * 1024
        ),
    )(
        initial_density.reshape(1024, 128),
        initial_thermal.reshape(1024, 128),
        boundary_mask.reshape(1024, 128),
        samples_a,
        samples_b,
        design_index,
    )
    return (
        first.reshape(GROUPS - 2, 4, 16, 128),
        total.reshape(GROUPS - 2, 4, 16, 128),
        variance.reshape(4, 16, 128),
    )


def solution(mesh):
    return jax.shard_map(
        local,
        mesh=mesh,
        in_specs=(
            P(None, "space", None),
            P(None, "space", None),
            P(None, "space", None),
            P(),
            P(),
            P(),
        ),
        out_specs=(
            P(None, "design", "space", None),
            P(None, "design", "space", None),
            P("design", "space", None),
        ),
        check_vma=False,
    )
```

```python
import jax
import jax.numpy as jnp
import numpy as np
from jax import lax
from jax.experimental import pallas as pl
from jax.experimental.pallas import tpu as pltpu
from jax.sharding import PartitionSpec as P

P_SIZE = 14
SAMPLES = 4
STEPS = 8
GROUPS = 16

HALO = 7
XS = 16
LAYERS = XS + 2 * HALO
ROWS = 40
PEERS = 8
MINE = 8
TILES = ROWS // 8
BLOCKS = (1, 1, 1, 1, 1, 1, 1)
LOG2E = float(np.log2(np.e))
MESH = pl.DeviceIdType.MESH


def take(tile, lanes):
    return jnp.take_along_axis(tile, lanes, axis=1, mode="promise_in_bounds")


def splat(value):
    return jnp.full((8, 128), value, jnp.float32)


def sample_coefficients(sa, sb, di, group, sample):
    picked = di[jnp.maximum(group - 2, 0)]
    t = []
    for p in range(P_SIZE):
        take_b = (group == 1) | ((group >= 2) & (picked == p))
        t.append(splat(jnp.where(take_b, sb[sample, p], sa[sample, p])))
    k0 = 0.04 + 0.06 * t[0]
    k1 = 0.5 + 0.5 * t[1]
    a = 0.02 + 0.04 * t[2]
    b2 = LOG2E * (1.0 + 3.0 * t[3])
    m = t[4]
    q = 0.2 + 0.6 * t[5]
    amb = 1.0 + 0.4 * t[6]
    h = 0.05 + 0.15 * t[7]
    ramp = 0.02 + 0.04 * t[8]
    src = 0.02 * t[9]
    wx = 0.5 + 0.5 * t[10]
    wz = 0.5 + 0.5 * t[11]
    gr = t[12]
    off = 0.3 * (t[13] - 0.5)
    c1 = k0 * k1
    inv = 1.0 / c1
    c0 = k0 * (0.5 + k1)
    lc1 = LOG2E * jnp.log(c1)
    first = LOG2E * jnp.log(a * LOG2E) + b2 * (amb - 1.0) - m * lc1
    return dict(
        wx=wx,
        wz=wz,
        wc=2.0 * (wx + wz + 1.0),
        p=b2 * (q - src) * inv,
        r=b2 * q * inv,
        k=b2 * (src * (1.0 - c0 * inv) - ramp),
        c0=c0,
        c1=c1,
        m=m,
        h=h,
        lc1=lc1,
        b2=b2,
        start=b2 * (off - amb),
        arg=first,
        arg_step=b2 * ramp - gr * (LOG2E / STEPS),
        out=10.0 * inv,
    )


def kernel(
    dens_ref,
    temp_ref,
    mask_ref,
    sa,
    sb,
    di,
    first_ref,
    total_ref,
    var_ref,
    t0,
    d0,
    m0,
    v0,
    u0,
    x0,
    y0,
    z0,
    theta_a,
    theta_b,
    u_ref,
    w_ref,
    h_ref,
    rsp,
    recv,
    halo_send,
    halo_recv,
    send_sem,
    recv_sem,
):
    d_index = lax.axis_index("design")
    s_index = lax.axis_index("space")
    s_count = lax.axis_size("space")
    zh = d_index // PEERS
    loc = d_index % PEERS
    right = (s_index + 1) % s_count
    left = (s_index + s_count - 1) % s_count

    def peer(j):
        return (loc + j) % PEERS

    barrier = pltpu.get_barrier_semaphore()
    for side in (left, right):
        pl.semaphore_signal(barrier, inc=1, device_id=(d_index, side), device_id_type=MESH)
    for j in range(1, PEERS):
        pl.semaphore_signal(
            barrier, inc=1, device_id=(zh * PEERS + peer(j), s_index), device_id_type=MESH
        )

    def stage(x, carry):
        for k in range(TILES):
            rows = pl.ds((24 * zh + 8 * k) * XS + x, 8, stride=XS)
            at = (HALO + x, pl.ds(8 * k, 8))
            t0[HALO + x, pl.ds(8 + 8 * k, 8)] = temp_ref[rows, :]
            d0[at] = dens_ref[rows, :]
            m0[at] = mask_ref[rows, :].astype(jnp.float32)
        return carry

    lax.fori_loop(0, XS, stage, 0)
    pl.semaphore_wait(barrier, PEERS + 1)

    halo = []
    for index, (ref, width) in enumerate(((t0, HALO), (d0, HALO - 1), (m0, HALO - 1))):
        for way, (source, target, side) in enumerate(
            ((HALO, HALO + XS, left), (HALO + XS - width, HALO - width, right))
        ):
            copy = pltpu.make_async_remote_copy(
                src_ref=ref.at[pl.ds(source, width)],
                dst_ref=ref.at[pl.ds(target, width)],
                send_sem=halo_send.at[2 * index + way],
                recv_sem=halo_recv.at[2 * index + way],
                device_id=(d_index, side),
                device_id_type=MESH,
            )
            copy.start()
            halo.append(copy)
    for copy in halo:
        copy.wait()

    thetas = (theta_a, theta_b)
    lane = lax.broadcasted_iota(jnp.int32, (8, 128), 1)
    row = lax.broadcasted_iota(jnp.int32, (8, 128), 0)
    lane_minus, lane_plus = jnp.maximum(lane - 1, 0), jnp.minimum(lane + 1, 127)
    row_first, row_last = row == 0, row == 7
    at_low = jnp.full((8, 128), s_index, jnp.int32) == 0
    at_high = jnp.full((8, 128), s_index, jnp.int32) == s_count - 1

    def y_sum(tile):
        return take(tile, lane_minus) + take(tile, lane_plus)

    def z_sum(ref, at, l, z, first, last):
        mid = ref[at + (l, pl.ds(8 + z, 8))]
        minus, plus = ref[at + (l, pl.ds(7 + z, 8))], ref[at + (l, pl.ds(9 + z, 8))]
        if first is not None:
            minus = jnp.where(first, mid, minus)
        if last is not None:
            plus = jnp.where(last, mid, plus)
        return minus + plus

    @pl.when(s_index == 0)
    def _():
        t0[HALO - 1] = jnp.zeros((ROWS + 16, 128), jnp.float32)

    @pl.when(s_index == s_count - 1)
    def _():
        t0[HALO + XS] = jnp.zeros((ROWS + 16, 128), jnp.float32)

    def prepare(b, carry):
        for j in range(4):
            l = 1 + 4 * b + j
            for k in range(TILES):
                at = (l, pl.ds(8 * k, 8))
                v = 1.0 - d0[at]
                v0[at] = v
                u0[at] = LOG2E * jnp.log(v)
                here = pl.ds(8 + 8 * k, 8)
                x0[at] = t0[l - 1, here] + t0[l + 1, here]
                z0[at] = z_sum(t0, (), l, 8 * k, row_first if k == 0 else None, row_last if k == TILES - 1 else None)
                y0[at] = y_sum(t0[l, here])
        return carry

    lax.fori_loop(0, (LAYERS - 2) // 4, prepare, 0)

    def evolve(i, carry):
        c = sample_coefficients(sa, sb, di, 2 * loc + i // SAMPLES, i % SAMPLES)

        for n in range(STEPS - 1):
            src, dst = n % 2, (n + 1) % 2
            last = n == STEPS - 2
            arg = c["arg"] + float(n) * c["arg_step"]
            if n == 0:
                arg = arg + c["m"] * c["lc1"]
            tiles = 4 if last else TILES
            low, layers = 1 + n, LAYERS - 2 - 2 * n
            blocks = BLOCKS[n]
            depth = -(-layers // blocks)
            depth_next = 0 if last else -(-(layers - 2) // BLOCKS[n + 1])
            parity = sum(BLOCKS[:n])

            def block(b, n=n, src=src, dst=dst, last=last, arg=arg, tiles=tiles, low=low, blocks=blocks, depth=depth, depth_next=depth_next, parity=parity):
                base = low + depth * b
                for k in range(tiles):
                    z = pl.multiple_of(8 * zh, 8) + 8 * k if last else 8 * k
                    here = pl.ds(8 + z, 8)
                    first_row = last_row = None
                    if k == 0:
                        first_row = row_first & (zh == 0) if last else row_first
                    if k == tiles - 1:
                        last_row = row_last & (zh == 1) if last else row_last
                    if n > 0:
                        column = [thetas[src][base - 1 + j, here] for j in range(depth + 2)]
                    for j in range(depth):
                        l = base + j
                        at = (l, pl.ds(z, 8))
                        if n == 0:
                            temp = t0[l, here]
                            laplace = c["b2"] * (
                                (c["wx"] * x0[at] + c["wz"] * z0[at]) + (y0[at] - c["wc"] * temp)
                            ) - c["p"]
                            mid = c["b2"] * temp + c["start"]
                            v, u = v0[at], u0[at]
                            conduct = c["c0"] - c["c1"] * v
                            new_u = (u + c["lc1"]) - jnp.exp2(mid + (c["m"] * u + arg))
                            keep = 1.0 - c["h"] * m0[at]
                            h_ref[at] = keep
                        else:
                            mid = column[j + 1]
                            laplace = (
                                c["wx"] * (column[j] + column[j + 2])
                                + c["wz"] * z_sum(thetas[src], (), l, z, first_row, last_row)
                            ) + (y_sum(mid) - (c["wc"] * mid + c["p"]))
                            u, conduct, keep = u_ref[at], w_ref[at], h_ref[at]
                            new_u = u - jnp.exp2(mid + (c["m"] * u + arg))
                        new_conduct = c["c0"] - jnp.exp2(new_u)
                        u_ref[at] = new_u
                        if not last:
                            w_ref[at] = new_conduct
                        new = keep * mid + conduct * laplace + (c["r"] * new_conduct + c["k"])
                        if n == 0 and l == HALO:
                            new = new - conduct * jnp.where(at_low, c["wx"] * c["start"], 0.0)
                        if n == 0 and l == HALO + XS - 1:
                            new = new - conduct * jnp.where(at_high, c["wx"] * c["start"], 0.0)
                        if l == HALO - 1:
                            new = jnp.where(at_low, 0.0, new)
                        if l == HALO + XS:
                            new = jnp.where(at_high, 0.0, new)
                        thetas[dst][l, here] = new

            block(0)

        arg = c["arg"] + float(STEPS - 1) * c["arg_step"]

        for x in range(XS):
            l = HALO + x
            for k in range(4):
                z = pl.multiple_of(8 * zh, 8) + 8 * k
                u = u_ref[l, pl.ds(z, 8)]
                new_u = u - jnp.exp2(theta_b[l, pl.ds(8 + z, 8)] + (c["m"] * u + arg))
                rsp[i, pl.ds(8 * k * XS + x, 8, stride=XS), :] = 10.0 - c["out"] * jnp.exp2(new_u)

        for j in range(1, PEERS):
            sends(i, j).start()
        own = pl.ds(pl.multiple_of(64 * loc, 8), 64)
        recv[loc * MINE + i] = rsp[i, own, :]
        return carry

    def sends(i, j):
        return pltpu.make_async_remote_copy(
            src_ref=rsp.at[i, pl.ds(pl.multiple_of(64 * peer(j), 8), 64)],
            dst_ref=recv.at[loc * MINE + i],
            send_sem=send_sem.at[i, j - 1],
            recv_sem=recv_sem.at[i, j - 1],
            device_id=(zh * PEERS + peer(j), s_index),
            device_id_type=MESH,
        )

    lax.fori_loop(0, MINE, evolve, 0)

    def drain(i, carry):
        for j in range(1, PEERS):
            sends(i, j).wait()
        return carry

    lax.fori_loop(0, MINE, drain, 0)

    def maps(tile, carry):
        at = pl.ds(pl.multiple_of(8 * tile, 8), 8)
        resp_a = [recv[s, at, :] for s in range(SAMPLES)]
        resp_b = [recv[SAMPLES + s, at, :] for s in range(SAMPLES)]
        pooled = resp_a + resp_b
        average = sum(pooled[1:], pooled[0]) * (1.0 / len(pooled))
        spread = [(r - average) * (r - average) for r in pooled]
        variance = sum(spread[1:], spread[0]) * (1.0 / len(pooled))
        var_ref[at, :] = variance
        for g in range(GROUPS - 2):
            first = total = None
            for s in range(SAMPLES):
                mixed = recv[(g + 2) * SAMPLES + s, at, :]
                to_b, to_a = resp_b[s] - mixed, resp_a[s] - mixed
                first = to_b * to_b if first is None else first + to_b * to_b
                total = to_a * to_a if total is None else total + to_a * to_a
            first_ref[g, at, :] = variance - (0.5 / SAMPLES) * first
            total_ref[g, at, :] = (0.5 / SAMPLES) * total
        return carry

    lax.fori_loop(0, 8, maps, 0)


def local(initial_density, initial_thermal, boundary_mask, samples_a, samples_b, design_index):
    vmem = pl.BlockSpec(memory_space=pltpu.VMEM)
    smem = pl.BlockSpec(memory_space=pltpu.SMEM)
    state = pltpu.VMEM((LAYERS, ROWS, 128), jnp.float32)
    responses = pltpu.VMEM((MINE, 512, 128), jnp.float32)
    dma = pltpu.SemaphoreType.DMA
    first, total, variance = pl.pallas_call(
        kernel,
        out_shape=(
            jax.ShapeDtypeStruct((GROUPS - 2, 64, 128), jnp.float32),
            jax.ShapeDtypeStruct((GROUPS - 2, 64, 128), jnp.float32),
            jax.ShapeDtypeStruct((64, 128), jnp.float32),
        ),
        in_specs=[vmem] * 3 + [smem] * 3,
        out_specs=(vmem, vmem, vmem),
        scratch_shapes=[
            pltpu.VMEM((LAYERS, ROWS + 16, 128), jnp.float32),
            state,
            state,
            state,
            state,
            state,
            state,
            state,
            pltpu.VMEM((LAYERS, ROWS + 16, 128), jnp.float32),
            pltpu.VMEM((LAYERS, ROWS + 16, 128), jnp.float32),
            state,
            state,
            state,
            responses,
            pltpu.VMEM((GROUPS * SAMPLES, 64, 128), jnp.float32),
            dma((6,)),
            dma((6,)),
            dma((MINE, PEERS - 1)),
            dma((MINE, PEERS - 1)),
        ],
        compiler_params=pltpu.CompilerParams(
            collective_id=0, has_side_effects=True, vmem_limit_bytes=32 * 1024 * 1024
        ),
    )(
        initial_density.reshape(1024, 128),
        initial_thermal.reshape(1024, 128),
        boundary_mask.reshape(1024, 128),
        samples_a,
        samples_b,
        design_index,
    )
    return (
        first.reshape(GROUPS - 2, 4, 16, 128),
        total.reshape(GROUPS - 2, 4, 16, 128),
        variance.reshape(4, 16, 128),
    )


def solution(mesh):
    return jax.shard_map(
        local,
        mesh=mesh,
        in_specs=(
            P(None, "space", None),
            P(None, "space", None),
            P(None, "space", None),
            P(),
            P(),
            P(),
        ),
        out_specs=(
            P(None, "design", "space", None),
            P(None, "design", "space", None),
            P("design", "space", None),
        ),
        check_vma=False,
    )
```

```python
import jax
import jax.numpy as jnp
import numpy as np
from jax import lax
from jax.experimental import pallas as pl
from jax.experimental.pallas import tpu as pltpu
from jax.sharding import PartitionSpec as P

P_SIZE = 14
SAMPLES = 4
STEPS = 8
GROUPS = 16

XS = 16
HALO = 7
LAYERS = XS + 2 * HALO
TILES = 5
ROWS = 8 * TILES
PEERS = 8
MINE = 8
LOG2E = float(np.log2(np.e))
MESH = pl.DeviceIdType.MESH


def take(tile, lanes):
    return jnp.take_along_axis(tile, lanes, axis=1, mode="promise_in_bounds")


def splat(value):
    return jnp.full((8, 128), value, jnp.float32)


def sample_coefficients(sa, sb, di, group, sample):
    picked = di[jnp.maximum(group - 2, 0)]
    t = []
    for p in range(P_SIZE):
        take_b = (group == 1) | ((group >= 2) & (picked == p))
        t.append(splat(jnp.where(take_b, sb[sample, p], sa[sample, p])))
    k0 = 0.04 + 0.06 * t[0]
    k1 = 0.5 + 0.5 * t[1]
    a = 0.02 + 0.04 * t[2]
    b2 = LOG2E * (1.0 + 3.0 * t[3])
    m = t[4]
    q = 0.2 + 0.6 * t[5]
    amb = 1.0 + 0.4 * t[6]
    h = 0.05 + 0.15 * t[7]
    ramp = 0.02 + 0.04 * t[8]
    src = 0.02 * t[9]
    wx = 0.5 + 0.5 * t[10]
    wz = 0.5 + 0.5 * t[11]
    gr = t[12]
    off = 0.3 * (t[13] - 0.5)
    c1 = k0 * k1
    inv = 1.0 / c1
    c0 = k0 * (0.5 + k1)
    lc1 = LOG2E * jnp.log(c1)
    return dict(
        wx=wx,
        wz=wz,
        wc=2.0 * (wx + wz + 1.0),
        p=b2 * (q - src) * inv,
        r=b2 * q * inv,
        k=b2 * (src * (1.0 - c0 * inv) - ramp),
        c0=c0,
        c1=c1,
        m=m,
        h=h,
        lc1=lc1,
        b2=b2,
        start=b2 * (off - amb),
        arg=LOG2E * jnp.log(a * LOG2E) + b2 * (amb - 1.0) - m * lc1,
        arg_step=b2 * ramp - gr * (LOG2E / STEPS),
        out=10.0 * inv,
    )


def kernel(
    dens_ref,
    temp_ref,
    mask_ref,
    sa_ref,
    sb_ref,
    di_ref,
    first_ref,
    total_ref,
    var_ref,
    raw_t,
    raw_d,
    raw_m,
    sa,
    sb,
    di,
    t0,
    d0,
    m0,
    v0,
    u0,
    x0,
    y0,
    z0,
    theta_a,
    theta_b,
    u_ref,
    w_ref,
    h_ref,
    rsp,
    recv,
    load_sem,
    halo_send,
    halo_recv,
    core_send,
    core_recv,
    send_sem,
    recv_sem,
):
    d_index = lax.axis_index("design")
    s_index = lax.axis_index("space")
    s_count = lax.axis_size("space")
    zh = d_index // PEERS
    loc = d_index % PEERS
    core = d_index % 2
    sibling = d_index + 1 - 2 * core
    right = (s_index + 1) % s_count
    left = (s_index + s_count - 1) % s_count
    zero_row = pl.multiple_of(8 * zh, 8)

    barrier = pltpu.get_barrier_semaphore()
    for side in (left, right):
        pl.semaphore_signal(barrier, inc=1, device_id=(d_index, side), device_id_type=MESH)
    for j in range(1, PEERS):
        pl.semaphore_signal(
            barrier,
            inc=1,
            device_id=(zh * PEERS + (loc + j) % PEERS, s_index),
            device_id_type=MESH,
        )

    here = pl.ds(pl.multiple_of(24 * XS * zh, 8), ROWS * XS)
    loads = [
        pltpu.make_async_copy(source, target, load_sem.at[index])
        for index, (source, target) in enumerate(
            (
                (temp_ref.at[here], raw_t),
                (dens_ref.at[here], raw_d),
                (mask_ref.at[here], raw_m),
                (sa_ref, sa),
                (sb_ref, sb),
                (di_ref, di),
            )
        )
    ]
    for load in loads:
        load.start()

    def stage(raw, target, shift):
        def layer(x, carry):
            for k in range(TILES):
                tile = raw[pl.ds(8 * k * XS + x, 8, stride=XS), :]
                target[HALO + x, pl.ds(shift + 8 * k, 8)] = tile.astype(jnp.float32)
            return carry

        lax.fori_loop(0, XS, layer, 0, unroll=4)

    for load, (raw, target, shift) in zip(loads, ((raw_t, t0, 8), (raw_d, d0, 0), (raw_m, m0, 0))):
        load.wait()
        stage(raw, target, shift)
    for load in loads[3:]:
        load.wait()

    pl.semaphore_wait(barrier, PEERS + 1)
    halo, handed = [], []
    for index, (ref, width, shift) in enumerate(
        ((t0, HALO, 8), (d0, HALO - 1, 0), (m0, HALO - 1, 0))
    ):
        rows = pl.ds(shift, ROWS)
        source = HALO + core * (XS - width)
        target = (1 - core) * (HALO + XS) + core * (HALO - width)
        halo.append(
            pltpu.make_async_remote_copy(
                src_ref=ref.at[pl.ds(source, width), rows],
                dst_ref=ref.at[pl.ds(target, width), rows],
                send_sem=halo_send.at[index],
                recv_sem=halo_recv.at[index],
                device_id=(d_index, (s_index + s_count - 1 + 2 * core) % s_count),
                device_id_type=MESH,
            )
        )
        handed.append(
            pltpu.make_async_remote_copy(
                src_ref=ref.at[pl.ds(target, width), rows],
                dst_ref=ref.at[pl.ds(target, width), rows],
                send_sem=core_send.at[index],
                recv_sem=core_recv.at[index],
                device_id=(sibling, s_index),
                device_id_type=MESH,
            )
        )
    for copy in halo:
        copy.start()

    thetas = (theta_a, theta_b)
    lane = lax.broadcasted_iota(jnp.int32, (8, 128), 1)
    row = lax.broadcasted_iota(jnp.int32, (8, 128), 0)
    lane_minus, lane_plus = jnp.maximum(lane - 1, 0), jnp.minimum(lane + 1, 127)
    row_first, row_last = row == 0, row == 7
    at_low = jnp.full((8, 128), s_index, jnp.int32) == 0
    at_high = jnp.full((8, 128), s_index, jnp.int32) == s_count - 1

    def y_sum(tile):
        return take(tile, lane_minus) + take(tile, lane_plus)

    def z_sum(tile_at, mid, z, first, last):
        minus, plus = tile_at(z - 1), tile_at(z + 1)
        if first is not None:
            minus = jnp.where(first, mid, minus)
        if last is not None:
            plus = jnp.where(last, mid, plus)
        return minus + plus

    def prepare(l):
        for k in range(TILES):
            at = (l, pl.ds(8 * k, 8))
            mid = t0[l, pl.ds(8 + 8 * k, 8)]
            v = 1.0 - d0[at]
            v0[at] = v
            u0[at] = LOG2E * jnp.log(v)
            x0[at] = t0[l - 1, pl.ds(8 + 8 * k, 8)] + t0[l + 1, pl.ds(8 + 8 * k, 8)]
            z0[at] = z_sum(
                lambda z: t0[l, pl.ds(8 + z, 8)],
                mid,
                8 * k,
                row_first if k == 0 else None,
                row_last if k == TILES - 1 else None,
            )
            y0[at] = y_sum(mid)

    def step(i, c, n, low, high):
        src, dst = thetas[n % 2], thetas[(n + 1) % 2]
        last = n == STEPS - 2
        arg = c["arg"] + float(n) * c["arg_step"]
        if n == 0:
            arg = arg + c["m"] * c["lc1"]
        tiles = 4 if last else TILES
        for k in range(tiles):
            z = zero_row + 8 * k if last else 8 * k
            rows = pl.ds(8 + z, 8)
            first_row = last_row = None
            if k == 0:
                first_row = row_first & (zh == 0) if last else row_first
            if k == tiles - 1:
                last_row = row_last & (zh == 1) if last else row_last
            for l in range(low, high + 1):
                at = (l, pl.ds(z, 8))
                own = (i, l, pl.ds(z, 8))
                if n == 0:
                    temp = t0[l, rows]
                    laplace = (
                        c["b2"] * ((c["wx"] * x0[at] + c["wz"] * z0[at]) + (y0[at] - c["wc"] * temp))
                        - c["p"]
                    )
                    mid = c["b2"] * temp + c["start"]
                    u = u0[at]
                    conduct = c["c0"] - c["c1"] * v0[at]
                    new_u = (u + c["lc1"]) - jnp.exp2(mid + (c["m"] * u + arg))
                    keep = 1.0 - c["h"] * m0[at]
                    h_ref[own] = keep
                else:
                    mid = src[i, l, rows]
                    laplace = (
                        c["wx"] * (src[i, l - 1, rows] + src[i, l + 1, rows])
                        + c["wz"]
                        * z_sum(lambda z: src[i, l, pl.ds(8 + z, 8)], mid, z, first_row, last_row)
                    ) + (y_sum(mid) - (c["wc"] * mid + c["p"]))
                    u, conduct, keep = u_ref[own], w_ref[own], h_ref[own]
                    new_u = u - jnp.exp2(mid + (c["m"] * u + arg))
                new_conduct = c["c0"] - jnp.exp2(new_u)
                u_ref[own] = new_u
                if not last:
                    w_ref[own] = new_conduct
                new = keep * mid + conduct * laplace + (c["r"] * new_conduct + c["k"])
                if n == 0 and l == HALO:
                    new = new - conduct * jnp.where(at_low, c["wx"] * c["start"], 0.0)
                if n == 0 and l == HALO + XS - 1:
                    new = new - conduct * jnp.where(at_high, c["wx"] * c["start"], 0.0)
                if l == HALO - 1:
                    new = jnp.where(at_low, 0.0, new)
                if l == HALO + XS:
                    new = jnp.where(at_high, 0.0, new)
                dst[i, l, rows] = new

    def coefficients_of(i):
        return sample_coefficients(sa, sb, di, 2 * loc + i // SAMPLES, i % SAMPLES)

    def inner(l, carry):
        prepare(HALO + 1 + 2 * l)
        prepare(HALO + 2 + 2 * l)
        return carry

    lax.fori_loop(0, (XS - 2) // 2, inner, 0)

    def ahead(i, carry):
        c = coefficients_of(i)
        for n in range(STEPS - 1):
            step(i, c, n, HALO + 1 + n, HALO + XS - 2 - n)
        for index, when in enumerate(HAND):

            @pl.when(i == when)
            def _(index=index):
                halo[index].wait_recv()
                handed[index].start()

        return carry

    lax.fori_loop(0, MINE, ahead, 0)
    for copy in halo:
        copy.wait_send()
    for copy in handed:
        copy.wait()

    @pl.when(s_index == 0)
    def _():
        t0[HALO - 1] = jnp.zeros((ROWS + 16, 128), jnp.float32)

    @pl.when(s_index == s_count - 1)
    def _():
        t0[HALO + XS] = jnp.zeros((ROWS + 16, 128), jnp.float32)

    def outer(l, carry):
        prepare(1 + l)
        prepare(HALO + XS - 1 + l)
        return carry

    lax.fori_loop(0, HALO, outer, 0)

    def sends(i, j):
        target = (loc + j) % PEERS
        return pltpu.make_async_remote_copy(
            src_ref=rsp.at[i, pl.ds(pl.multiple_of(64 * target, 8), 64)],
            dst_ref=recv.at[loc * MINE + i],
            send_sem=send_sem.at[i, j - 1],
            recv_sem=recv_sem.at[i, j - 1],
            device_id=(zh * PEERS + target, s_index),
            device_id_type=MESH,
        )

    def rest(i, carry):
        c = coefficients_of(i)
        for n in range(STEPS - 1):
            step(i, c, n, 1 + n, HALO + n)
            step(i, c, n, HALO + XS - 1 - n, LAYERS - 2 - n)
        arg = c["arg"] + float(STEPS - 1) * c["arg_step"]
        for x in range(XS):
            l = HALO + x
            for k in range(4):
                z = zero_row + 8 * k
                u = u_ref[i, l, pl.ds(z, 8)]
                new_u = u - jnp.exp2(theta_b[i, l, pl.ds(8 + z, 8)] + (c["m"] * u + arg))
                rsp[i, pl.ds(8 * k * XS + x, 8, stride=XS), :] = 10.0 - c["out"] * jnp.exp2(new_u)
        for j in range(1, PEERS):
            sends(i, j).start()
        recv[loc * MINE + i] = rsp[i, pl.ds(pl.multiple_of(64 * loc, 8), 64), :]
        return carry

    lax.fori_loop(0, MINE, rest, 0)

    def drain(i, carry):
        for j in range(1, PEERS):
            sends(i, j).wait()
        return carry

    lax.fori_loop(0, MINE, drain, 0)

    def maps(tile, carry):
        at = pl.ds(pl.multiple_of(8 * tile, 8), 8)
        resp_a = [recv[s, at, :] for s in range(SAMPLES)]
        resp_b = [recv[SAMPLES + s, at, :] for s in range(SAMPLES)]
        pooled = resp_a + resp_b
        average = sum(pooled[1:], pooled[0]) * (1.0 / len(pooled))
        spread = [(r - average) * (r - average) for r in pooled]
        variance = sum(spread[1:], spread[0]) * (1.0 / len(pooled))
        var_ref[at, :] = variance
        for g in range(GROUPS - 2):
            first = total = None
            for s in range(SAMPLES):
                mixed = recv[(g + 2) * SAMPLES + s, at, :]
                to_b, to_a = resp_b[s] - mixed, resp_a[s] - mixed
                first = to_b * to_b if first is None else first + to_b * to_b
                total = to_a * to_a if total is None else total + to_a * to_a
            first_ref[g, at, :] = variance - (0.5 / SAMPLES) * first
            total_ref[g, at, :] = (0.5 / SAMPLES) * total
        return carry

    lax.fori_loop(0, 8, maps, 0)


HAND = (3, 5, 6)


def local(initial_density, initial_thermal, boundary_mask, samples_a, samples_b, design_index):
    vmem = pl.BlockSpec(memory_space=pltpu.VMEM)
    hbm = pl.BlockSpec(memory_space=pl.ANY)
    dma = pltpu.SemaphoreType.DMA

    def state(*shape):
        return pltpu.VMEM(shape + (128,), jnp.float32)

    first, total, variance = pl.pallas_call(
        kernel,
        out_shape=(
            jax.ShapeDtypeStruct((GROUPS - 2, 64, 128), jnp.float32),
            jax.ShapeDtypeStruct((GROUPS - 2, 64, 128), jnp.float32),
            jax.ShapeDtypeStruct((64, 128), jnp.float32),
        ),
        in_specs=[hbm] * 6,
        out_specs=(vmem, vmem, vmem),
        scratch_shapes=[
            state(ROWS * XS),
            state(ROWS * XS),
            pltpu.VMEM((ROWS * XS, 128), jnp.int32),
            pltpu.SMEM((SAMPLES, P_SIZE), jnp.float32),
            pltpu.SMEM((SAMPLES, P_SIZE), jnp.float32),
            pltpu.SMEM((P_SIZE,), jnp.int32),
            state(LAYERS, ROWS + 16),
        ]
        + [state(LAYERS, ROWS)] * 7
        + [state(MINE, LAYERS, ROWS + 16)] * 2
        + [state(MINE, LAYERS, ROWS)] * 3
        + [
            state(MINE, 512),
            state(GROUPS * SAMPLES, 64),
            dma((6,)),
            dma((3,)),
            dma((3,)),
            dma((3,)),
            dma((3,)),
            dma((MINE, PEERS - 1)),
            dma((MINE, PEERS - 1)),
        ],
        compiler_params=pltpu.CompilerParams(
            collective_id=0, has_side_effects=True, vmem_limit_bytes=48 * 1024 * 1024
        ),
    )(
        initial_density.reshape(1024, 128),
        initial_thermal.reshape(1024, 128),
        boundary_mask.reshape(1024, 128),
        samples_a,
        samples_b,
        design_index,
    )
    return (
        first.reshape(GROUPS - 2, 4, 16, 128),
        total.reshape(GROUPS - 2, 4, 16, 128),
        variance.reshape(4, 16, 128),
    )


def solution(mesh):
    return jax.shard_map(
        local,
        mesh=mesh,
        in_specs=(
            P(None, "space", None),
            P(None, "space", None),
            P(None, "space", None),
            P(),
            P(),
            P(),
        ),
        out_specs=(
            P(None, "design", "space", None),
            P(None, "design", "space", None),
            P("design", "space", None),
        ),
        check_vma=False,
    )
```

```python
import jax
import jax.numpy as jnp
import numpy as np
from jax import lax
from jax.experimental import pallas as pl
from jax.experimental.pallas import tpu as pltpu
from jax.sharding import PartitionSpec as P

P_SIZE = 14
SAMPLES = 4
STEPS = 8
GROUPS = 16

XS = 16
HALO = 7
LAYERS = XS + 2 * HALO
TILES = 5
ROWS = 8 * TILES
PEERS = 8
MINE = 8
LOG2E = float(np.log2(np.e))
MESH = pl.DeviceIdType.MESH


def take(tile, lanes):
    return jnp.take_along_axis(tile, lanes, axis=1, mode="promise_in_bounds")


def splat(value):
    return jnp.full((8, 128), value, jnp.float32)


def sample_coefficients(sa, sb, di, group, sample):
    picked = di[jnp.maximum(group - 2, 0)]
    t = []
    for p in range(P_SIZE):
        take_b = (group == 1) | ((group >= 2) & (picked == p))
        t.append(splat(jnp.where(take_b, sb[sample, p], sa[sample, p])))
    k0 = 0.04 + 0.06 * t[0]
    k1 = 0.5 + 0.5 * t[1]
    a = 0.02 + 0.04 * t[2]
    b2 = LOG2E * (1.0 + 3.0 * t[3])
    m = t[4]
    q = 0.2 + 0.6 * t[5]
    amb = 1.0 + 0.4 * t[6]
    h = 0.05 + 0.15 * t[7]
    ramp = 0.02 + 0.04 * t[8]
    src = 0.02 * t[9]
    wx = 0.5 + 0.5 * t[10]
    wz = 0.5 + 0.5 * t[11]
    gr = t[12]
    off = 0.3 * (t[13] - 0.5)
    c1 = k0 * k1
    inv = 1.0 / c1
    c0 = k0 * (0.5 + k1)
    lc1 = LOG2E * jnp.log(c1)
    return dict(
        wx=wx,
        wz=wz,
        wc=2.0 * (wx + wz + 1.0),
        p=b2 * (q - src) * inv,
        r=b2 * q * inv,
        k=b2 * (src * (1.0 - c0 * inv) - ramp),
        c0=c0,
        c1=c1,
        m=m,
        h=h,
        lc1=lc1,
        b2=b2,
        start=b2 * (off - amb),
        arg=LOG2E * jnp.log(a * LOG2E) + b2 * (amb - 1.0) - m * lc1,
        arg_step=b2 * ramp - gr * (LOG2E / STEPS),
        out=10.0 * inv,
    )


def kernel(
    dens_ref,
    temp_ref,
    mask_ref,
    sa_ref,
    sb_ref,
    di_ref,
    first_ref,
    total_ref,
    var_ref,
    raw_t,
    raw_d,
    raw_m,
    sa,
    sb,
    di,
    t0,
    d0,
    m0,
    v0,
    u0,
    x0,
    y0,
    z0,
    theta_a,
    theta_b,
    u_ref,
    w_ref,
    h_ref,
    rsp,
    recv,
    load_sem,
    halo_send,
    halo_recv,
    core_send,
    core_recv,
    send_sem,
    recv_sem,
):
    d_index = lax.axis_index("design")
    s_index = lax.axis_index("space")
    s_count = lax.axis_size("space")
    zh = d_index // PEERS
    loc = d_index % PEERS
    core = d_index % 2
    sibling = d_index + 1 - 2 * core
    right = (s_index + 1) % s_count
    left = (s_index + s_count - 1) % s_count
    zero_row = pl.multiple_of(8 * zh, 8)

    barrier = pltpu.get_barrier_semaphore()
    for side in (left, right):
        pl.semaphore_signal(barrier, inc=1, device_id=(d_index, side), device_id_type=MESH)
    for j in range(1, PEERS):
        pl.semaphore_signal(
            barrier,
            inc=1,
            device_id=(zh * PEERS + (loc + j) % PEERS, s_index),
            device_id_type=MESH,
        )

    here = pl.ds(pl.multiple_of(24 * XS * zh, 8), ROWS * XS)
    loads = [
        pltpu.make_async_copy(source, target, load_sem.at[index])
        for index, (source, target) in enumerate(
            (
                (temp_ref.at[here], raw_t),
                (dens_ref.at[here], raw_d),
                (mask_ref.at[here], raw_m),
                (sa_ref, sa),
                (sb_ref, sb),
                (di_ref, di),
            )
        )
    ]
    for load in loads:
        load.start()

    def stage(raw, target, shift):
        def layer(x, carry):
            for k in range(TILES):
                tile = raw[pl.ds(8 * k * XS + x, 8, stride=XS), :]
                target[HALO + x, pl.ds(shift + 8 * k, 8)] = tile.astype(jnp.float32)
            return carry

        lax.fori_loop(0, XS, layer, 0, unroll=4)

    for load, (raw, target, shift) in zip(loads, ((raw_t, t0, 8), (raw_d, d0, 0), (raw_m, m0, 0))):
        load.wait()
        stage(raw, target, shift)
    for load in loads[3:]:
        load.wait()

    pl.semaphore_wait(barrier, PEERS + 1)
    halo, handed = [], []
    for index, (ref, width, shift) in enumerate(
        ((t0, HALO, 8), (d0, HALO - 1, 0), (m0, HALO - 1, 0))
    ):
        rows = pl.ds(shift, ROWS)
        source = HALO + core * (XS - width)
        target = (1 - core) * (HALO + XS) + core * (HALO - width)
        halo.append(
            pltpu.make_async_remote_copy(
                src_ref=ref.at[pl.ds(source, width), rows],
                dst_ref=ref.at[pl.ds(target, width), rows],
                send_sem=halo_send.at[index],
                recv_sem=halo_recv.at[index],
                device_id=(d_index, (s_index + s_count - 1 + 2 * core) % s_count),
                device_id_type=MESH,
            )
        )
        handed.append(
            pltpu.make_async_remote_copy(
                src_ref=ref.at[pl.ds(target, width), rows],
                dst_ref=ref.at[pl.ds(target, width), rows],
                send_sem=core_send.at[index],
                recv_sem=core_recv.at[index],
                device_id=(sibling, s_index),
                device_id_type=MESH,
            )
        )
    for copy in halo:
        copy.start()

    thetas = (theta_a, theta_b)
    lane = lax.broadcasted_iota(jnp.int32, (8, 128), 1)
    row = lax.broadcasted_iota(jnp.int32, (8, 128), 0)
    lane_minus, lane_plus = jnp.maximum(lane - 1, 0), jnp.minimum(lane + 1, 127)
    row_first, row_last = row == 0, row == 7
    at_low = jnp.full((8, 128), s_index, jnp.int32) == 0
    at_high = jnp.full((8, 128), s_index, jnp.int32) == s_count - 1

    def y_sum(tile):
        return take(tile, lane_minus) + take(tile, lane_plus)

    def z_sum(tile_at, mid, z, first, last):
        minus, plus = tile_at(z - 1), tile_at(z + 1)
        if first is not None:
            minus = jnp.where(first, mid, minus)
        if last is not None:
            plus = jnp.where(last, mid, plus)
        return minus + plus

    def prepare(l):
        for k in range(TILES):
            at = (l, pl.ds(8 * k, 8))
            mid = t0[l, pl.ds(8 + 8 * k, 8)]
            v = 1.0 - d0[at]
            v0[at] = v
            u0[at] = LOG2E * jnp.log(v)
            x0[at] = t0[l - 1, pl.ds(8 + 8 * k, 8)] + t0[l + 1, pl.ds(8 + 8 * k, 8)]
            z0[at] = z_sum(
                lambda z: t0[l, pl.ds(8 + z, 8)],
                mid,
                8 * k,
                row_first if k == 0 else None,
                row_last if k == TILES - 1 else None,
            )
            y0[at] = y_sum(mid)

    def step(i, c, n, low, high):
        src, dst = thetas[n % 2], thetas[(n + 1) % 2]
        last = n == STEPS - 2
        arg = c["arg"] + float(n) * c["arg_step"]
        if n == 0:
            arg = arg + c["m"] * c["lc1"]
        tiles = 4 if last else TILES
        for k in range(tiles):
            z = zero_row + 8 * k if last else 8 * k
            rows = pl.ds(8 + z, 8)
            first_row = last_row = None
            if k == 0:
                first_row = row_first & (zh == 0) if last else row_first
            if k == tiles - 1:
                last_row = row_last & (zh == 1) if last else row_last
            for l in range(low, high + 1):
                at = (l, pl.ds(z, 8))
                own = (i, l, pl.ds(z, 8))
                if n == 0:
                    temp = t0[l, rows]
                    laplace = (
                        c["b2"] * ((c["wx"] * x0[at] + c["wz"] * z0[at]) + (y0[at] - c["wc"] * temp))
                        - c["p"]
                    )
                    mid = c["b2"] * temp + c["start"]
                    u = u0[at]
                    conduct = c["c0"] - c["c1"] * v0[at]
                    new_u = (u + c["lc1"]) - jnp.exp2(mid + (c["m"] * u + arg))
                    keep = 1.0 - c["h"] * m0[at]
                    h_ref[own] = keep
                else:
                    mid = src[i, l, rows]
                    laplace = (
                        c["wx"] * (src[i, l - 1, rows] + src[i, l + 1, rows])
                        + c["wz"]
                        * z_sum(lambda z: src[i, l, pl.ds(8 + z, 8)], mid, z, first_row, last_row)
                    ) + (y_sum(mid) - (c["wc"] * mid + c["p"]))
                    u, conduct, keep = u_ref[own], w_ref[own], h_ref[own]
                    new_u = u - jnp.exp2(mid + (c["m"] * u + arg))
                new_conduct = c["c0"] - jnp.exp2(new_u)
                u_ref[own] = new_u
                if not last:
                    w_ref[own] = new_conduct
                new = keep * mid + conduct * laplace + (c["r"] * new_conduct + c["k"])
                if n == 0 and l == HALO:
                    new = new - conduct * jnp.where(at_low, c["wx"] * c["start"], 0.0)
                if n == 0 and l == HALO + XS - 1:
                    new = new - conduct * jnp.where(at_high, c["wx"] * c["start"], 0.0)
                if l == HALO - 1:
                    new = jnp.where(at_low, 0.0, new)
                if l == HALO + XS:
                    new = jnp.where(at_high, 0.0, new)
                dst[i, l, rows] = new

    def coefficients_of(i):
        return sample_coefficients(sa, sb, di, 2 * loc + i // SAMPLES, i % SAMPLES)

    def inner(l, carry):
        prepare(HALO + 1 + 2 * l)
        prepare(HALO + 2 + 2 * l)
        return carry

    lax.fori_loop(0, (XS - 2) // 2, inner, 0)

    def ahead(i, carry):
        c = coefficients_of(i)
        for n in range(STEPS - 1):
            step(i, c, n, HALO + 1 + n, HALO + XS - 2 - n)
        for index, when in enumerate(HAND):

            @pl.when(i == when)
            def _(index=index):
                halo[index].wait_recv()
                handed[index].start()

        return carry

    lax.fori_loop(0, MINE, ahead, 0)
    for copy in halo:
        copy.wait_send()
    for copy in handed:
        copy.wait()

    @pl.when(s_index == 0)
    def _():
        t0[HALO - 1] = jnp.zeros((ROWS + 16, 128), jnp.float32)

    @pl.when(s_index == s_count - 1)
    def _():
        t0[HALO + XS] = jnp.zeros((ROWS + 16, 128), jnp.float32)

    def outer(l, carry):
        prepare(1 + l)
        prepare(HALO + XS - 1 + l)
        return carry

    lax.fori_loop(0, HALO, outer, 0)

    def sends(i, j):
        target = (loc + j) % PEERS
        return pltpu.make_async_remote_copy(
            src_ref=rsp.at[i, pl.ds(pl.multiple_of(64 * target, 8), 64)],
            dst_ref=recv.at[loc * MINE + i],
            send_sem=send_sem.at[i, j - 1],
            recv_sem=recv_sem.at[i, j - 1],
            device_id=(zh * PEERS + target, s_index),
            device_id_type=MESH,
        )

    def rest(i, carry):
        c = coefficients_of(i)
        for n in range(STEPS - 1):
            step(i, c, n, 1 + n, HALO + n)
            step(i, c, n, HALO + XS - 1 - n, LAYERS - 2 - n)
        arg = c["arg"] + float(STEPS - 1) * c["arg_step"]
        for x in range(XS):
            l = HALO + x
            for k in range(4):
                z = zero_row + 8 * k
                u = u_ref[i, l, pl.ds(z, 8)]
                new_u = u - jnp.exp2(theta_b[i, l, pl.ds(8 + z, 8)] + (c["m"] * u + arg))
                rsp[i, pl.ds(8 * k * XS + x, 8, stride=XS), :] = 10.0 - c["out"] * jnp.exp2(new_u)
        for j in range(1, PEERS):
            sends(i, j).start()
        recv[loc * MINE + i] = rsp[i, pl.ds(pl.multiple_of(64 * loc, 8), 64), :]
        return carry

    lax.fori_loop(0, MINE, rest, 0)

    def drain(i, carry):
        for j in range(1, PEERS):
            sends(i, j).wait()
        return carry

    lax.fori_loop(0, MINE, drain, 0)

    def maps(tile, carry):
        at = pl.ds(pl.multiple_of(8 * tile, 8), 8)
        resp_a = [recv[s, at, :] for s in range(SAMPLES)]
        resp_b = [recv[SAMPLES + s, at, :] for s in range(SAMPLES)]
        pooled = resp_a + resp_b
        average = sum(pooled[1:], pooled[0]) * (1.0 / len(pooled))
        spread = [(r - average) * (r - average) for r in pooled]
        variance = sum(spread[1:], spread[0]) * (1.0 / len(pooled))
        var_ref[at, :] = variance
        for g in range(GROUPS - 2):
            first = total = None
            for s in range(SAMPLES):
                mixed = recv[(g + 2) * SAMPLES + s, at, :]
                to_b, to_a = resp_b[s] - mixed, resp_a[s] - mixed
                first = to_b * to_b if first is None else first + to_b * to_b
                total = to_a * to_a if total is None else total + to_a * to_a
            first_ref[g, at, :] = variance - (0.5 / SAMPLES) * first
            total_ref[g, at, :] = (0.5 / SAMPLES) * total
        return carry

    lax.fori_loop(0, 8, maps, 0)


HAND = (3, 5, 6)


def local(initial_density, initial_thermal, boundary_mask, samples_a, samples_b, design_index):
    vmem = pl.BlockSpec(memory_space=pltpu.VMEM)
    hbm = pl.BlockSpec(memory_space=pl.ANY)
    dma = pltpu.SemaphoreType.DMA

    def state(*shape):
        return pltpu.VMEM(shape + (128,), jnp.float32)

    first, total, variance = pl.pallas_call(
        kernel,
        out_shape=(
            jax.ShapeDtypeStruct((GROUPS - 2, 64, 128), jnp.float32),
            jax.ShapeDtypeStruct((GROUPS - 2, 64, 128), jnp.float32),
            jax.ShapeDtypeStruct((64, 128), jnp.float32),
        ),
        in_specs=[hbm] * 6,
        out_specs=(vmem, vmem, vmem),
        scratch_shapes=[
            state(ROWS * XS),
            state(ROWS * XS),
            pltpu.VMEM((ROWS * XS, 128), jnp.int32),
            pltpu.SMEM((SAMPLES, P_SIZE), jnp.float32),
            pltpu.SMEM((SAMPLES, P_SIZE), jnp.float32),
            pltpu.SMEM((P_SIZE,), jnp.int32),
            state(LAYERS, ROWS + 16),
        ]
        + [state(LAYERS, ROWS)] * 7
        + [state(MINE, LAYERS, ROWS + 16)] * 2
        + [state(MINE, LAYERS, ROWS)] * 3
        + [
            state(MINE, 512),
            state(GROUPS * SAMPLES, 64),
            dma((6,)),
            dma((3,)),
            dma((3,)),
            dma((3,)),
            dma((3,)),
            dma((MINE, PEERS - 1)),
            dma((MINE, PEERS - 1)),
        ],
        compiler_params=pltpu.CompilerParams(
            collective_id=0, has_side_effects=True, vmem_limit_bytes=54067 * 1024
        ),
    )(
        initial_density.reshape(1024, 128),
        initial_thermal.reshape(1024, 128),
        boundary_mask.reshape(1024, 128),
        samples_a,
        samples_b,
        design_index,
    )
    return (
        first.reshape(GROUPS - 2, 4, 16, 128),
        total.reshape(GROUPS - 2, 4, 16, 128),
        variance.reshape(4, 16, 128),
    )


def solution(mesh):
    return jax.shard_map(
        local,
        mesh=mesh,
        in_specs=(
            P(None, "space", None),
            P(None, "space", None),
            P(None, "space", None),
            P(),
            P(),
            P(),
        ),
        out_specs=(
            P(None, "design", "space", None),
            P(None, "design", "space", None),
            P("design", "space", None),
        ),
        check_vma=False,
    )
```

```python
import jax
import jax.numpy as jnp
import numpy as np
from jax import lax
from jax.experimental import pallas as pl
from jax.experimental.pallas import tpu as pltpu
from jax.sharding import PartitionSpec as P

P_SIZE = 14
SAMPLES = 4
STEPS = 8
GROUPS = 16

XS = 16
HALO = 7
LAYERS = XS + 2 * HALO
TILES = 5
ROWS = 8 * TILES
PEERS = 8
MINE = 8
LOG2E = float(np.log2(np.e))
MESH = pl.DeviceIdType.MESH


def take(tile, lanes):
    return jnp.take_along_axis(tile, lanes, axis=1, mode="promise_in_bounds")


def splat(value):
    return jnp.full((8, 128), value, jnp.float32)


def sample_coefficients(sa, sb, di, group, sample):
    picked = di[jnp.maximum(group - 2, 0)]
    t = []
    for p in range(P_SIZE):
        take_b = (group == 1) | ((group >= 2) & (picked == p))
        t.append(splat(jnp.where(take_b, sb[sample, p], sa[sample, p])))
    k0 = 0.04 + 0.06 * t[0]
    k1 = 0.5 + 0.5 * t[1]
    a = 0.02 + 0.04 * t[2]
    b2 = LOG2E * (1.0 + 3.0 * t[3])
    m = t[4]
    q = 0.2 + 0.6 * t[5]
    amb = 1.0 + 0.4 * t[6]
    h = 0.05 + 0.15 * t[7]
    ramp = 0.02 + 0.04 * t[8]
    src = 0.02 * t[9]
    wx = 0.5 + 0.5 * t[10]
    wz = 0.5 + 0.5 * t[11]
    gr = t[12]
    off = 0.3 * (t[13] - 0.5)
    c1 = k0 * k1
    inv = 1.0 / c1
    c0 = k0 * (0.5 + k1)
    lc1 = LOG2E * jnp.log(c1)
    return dict(
        wx=wx,
        wz=wz,
        wc=2.0 * (wx + wz + 1.0),
        p=b2 * (q - src) * inv,
        r=b2 * q * inv,
        k=b2 * (src * (1.0 - c0 * inv) - ramp),
        c0=c0,
        c1=c1,
        m=m,
        h=h,
        lc1=lc1,
        b2=b2,
        start=b2 * (off - amb),
        arg=LOG2E * jnp.log(a * LOG2E) + b2 * (amb - 1.0) - m * lc1,
        arg_step=b2 * ramp - gr * (LOG2E / STEPS),
        out=10.0 * inv,
    )


def kernel(
    dens_ref,
    temp_ref,
    mask_ref,
    sa_ref,
    sb_ref,
    di_ref,
    first_ref,
    total_ref,
    var_ref,
    raw_t,
    raw_d,
    raw_m,
    sa,
    sb,
    di,
    t0,
    d0,
    m0,
    v0,
    u0,
    x0,
    y0,
    z0,
    theta_a,
    theta_b,
    u_ref,
    w_ref,
    h_ref,
    rsp,
    extra,
    recv,
    load_sem,
    halo_send,
    halo_recv,
    core_send,
    core_recv,
    send_sem,
    recv_sem,
    extra_send,
    extra_recv,
):
    d_index = lax.axis_index("design")
    s_index = lax.axis_index("space")
    s_count = lax.axis_size("space")
    zh = d_index // PEERS
    loc = d_index % PEERS
    core = d_index % 2
    y = loc // 2
    sibling = d_index + 1 - 2 * core
    right = (s_index + 1) % s_count
    left = (s_index + s_count - 1) % s_count
    zero_row = pl.multiple_of(8 * zh, 8)

    barrier = pltpu.get_barrier_semaphore()
    for side in (left, right):
        pl.semaphore_signal(barrier, inc=1, device_id=(d_index, side), device_id_type=MESH)
    for j in range(1, PEERS):
        pl.semaphore_signal(
            barrier,
            inc=1,
            device_id=(zh * PEERS + (loc + j) % PEERS, s_index),
            device_id_type=MESH,
        )

    here = pl.ds(pl.multiple_of(24 * XS * zh, 8), ROWS * XS)
    loads = [
        pltpu.make_async_copy(source, target, load_sem.at[index])
        for index, (source, target) in enumerate(
            (
                (temp_ref.at[here], raw_t),
                (dens_ref.at[here], raw_d),
                (mask_ref.at[here], raw_m),
                (sa_ref, sa),
                (sb_ref, sb),
                (di_ref, di),
            )
        )
    ]
    for load in loads:
        load.start()

    def stage(raw, target, shift):
        def layer(x, carry):
            for k in range(TILES):
                tile = raw[pl.ds(8 * k * XS + x, 8, stride=XS), :]
                target[HALO + x, pl.ds(shift + 8 * k, 8)] = tile.astype(jnp.float32)
            return carry

        lax.fori_loop(0, XS, layer, 0, unroll=4)

    for load, (raw, target, shift) in zip(loads, ((raw_t, t0, 8), (raw_d, d0, 0), (raw_m, m0, 0))):
        load.wait()
        stage(raw, target, shift)
    for load in loads[3:]:
        load.wait()

    pl.semaphore_wait(barrier, PEERS + 1)
    halo, handed = [], []
    for index, (ref, width, shift) in enumerate(
        ((t0, HALO, 8), (d0, HALO - 1, 0), (m0, HALO - 1, 0))
    ):
        rows = pl.ds(shift, ROWS)
        source = HALO + core * (XS - width)
        target = (1 - core) * (HALO + XS) + core * (HALO - width)
        halo.append(
            pltpu.make_async_remote_copy(
                src_ref=ref.at[pl.ds(source, width), rows],
                dst_ref=ref.at[pl.ds(target, width), rows],
                send_sem=halo_send.at[index],
                recv_sem=halo_recv.at[index],
                device_id=(d_index, (s_index + s_count - 1 + 2 * core) % s_count),
                device_id_type=MESH,
            )
        )
        handed.append(
            pltpu.make_async_remote_copy(
                src_ref=ref.at[pl.ds(target, width), rows],
                dst_ref=ref.at[pl.ds(target, width), rows],
                send_sem=core_send.at[index],
                recv_sem=core_recv.at[index],
                device_id=(sibling, s_index),
                device_id_type=MESH,
            )
        )
    for copy in halo:
        copy.start()

    thetas = (theta_a, theta_b)
    lane = lax.broadcasted_iota(jnp.int32, (8, 128), 1)
    row = lax.broadcasted_iota(jnp.int32, (8, 128), 0)
    lane_minus, lane_plus = jnp.maximum(lane - 1, 0), jnp.minimum(lane + 1, 127)
    row_first, row_last = row == 0, row == 7
    at_low = jnp.full((8, 128), s_index, jnp.int32) == 0
    at_high = jnp.full((8, 128), s_index, jnp.int32) == s_count - 1

    def y_sum(tile):
        return take(tile, lane_minus) + take(tile, lane_plus)

    def z_sum(tile_at, mid, z, first, last):
        minus, plus = tile_at(z - 1), tile_at(z + 1)
        if first is not None:
            minus = jnp.where(first, mid, minus)
        if last is not None:
            plus = jnp.where(last, mid, plus)
        return minus + plus

    def prepare(l):
        for k in range(TILES):
            at = (l, pl.ds(8 * k, 8))
            mid = t0[l, pl.ds(8 + 8 * k, 8)]
            v = 1.0 - d0[at]
            v0[at] = v
            u0[at] = LOG2E * jnp.log(v)
            x0[at] = t0[l - 1, pl.ds(8 + 8 * k, 8)] + t0[l + 1, pl.ds(8 + 8 * k, 8)]
            z0[at] = z_sum(
                lambda z: t0[l, pl.ds(8 + z, 8)],
                mid,
                8 * k,
                row_first if k == 0 else None,
                row_last if k == TILES - 1 else None,
            )
            y0[at] = y_sum(mid)

    def step(i, c, n, low, high, base, tiles, at_start=None, at_end=None):
        src, dst = thetas[n % 2], thetas[(n + 1) % 2]
        arg = c["arg"] + float(n) * c["arg_step"]
        if n == 0:
            arg = arg + c["m"] * c["lc1"]
        for k in range(tiles):
            z = base + 8 * k
            rows = pl.ds(8 + z, 8)
            first_row = last_row = None
            if k == 0:
                first_row = row_first if at_start is None else row_first & at_start
            if k == tiles - 1:
                last_row = row_last if at_end is None else row_last & at_end
            for l in range(low, high + 1):
                at = (l, pl.ds(z, 8))
                own = (i, l, pl.ds(z, 8))
                if n == 0:
                    temp = t0[l, rows]
                    laplace = (
                        c["b2"] * ((c["wx"] * x0[at] + c["wz"] * z0[at]) + (y0[at] - c["wc"] * temp))
                        - c["p"]
                    )
                    mid = c["b2"] * temp + c["start"]
                    u = u0[at]
                    conduct = c["c0"] - c["c1"] * v0[at]
                    new_u = (u + c["lc1"]) - jnp.exp2(mid + (c["m"] * u + arg))
                    keep = 1.0 - c["h"] * m0[at]
                    h_ref[own] = keep
                else:
                    mid = src[i, l, rows]
                    laplace = (
                        c["wx"] * (src[i, l - 1, rows] + src[i, l + 1, rows])
                        + c["wz"]
                        * z_sum(lambda z: src[i, l, pl.ds(8 + z, 8)], mid, z, first_row, last_row)
                    ) + (y_sum(mid) - (c["wc"] * mid + c["p"]))
                    u, conduct, keep = u_ref[own], w_ref[own], h_ref[own]
                    new_u = u - jnp.exp2(mid + (c["m"] * u + arg))
                new_conduct = c["c0"] - jnp.exp2(new_u)
                u_ref[own] = new_u
                if n < STEPS - 2:
                    w_ref[own] = new_conduct
                new = keep * mid + conduct * laplace + (c["r"] * new_conduct + c["k"])
                if n == 0 and l == HALO:
                    new = new - conduct * jnp.where(at_low, c["wx"] * c["start"], 0.0)
                if n == 0 and l == HALO + XS - 1:
                    new = new - conduct * jnp.where(at_high, c["wx"] * c["start"], 0.0)
                if l == HALO - 1:
                    new = jnp.where(at_low, 0.0, new)
                if l == HALO + XS:
                    new = jnp.where(at_high, 0.0, new)
                dst[i, l, rows] = new

    def main_step(i, c, n, low, high):
        if n < STEPS - 2:
            step(i, c, n, low, high, 0, TILES)
        else:
            step(i, c, n, low, high, zero_row, 4, zh == 0, zh == 1)

    def coefficients_of(owner, i):
        return sample_coefficients(sa, sb, di, 2 * owner + i // SAMPLES, i % SAMPLES)

    def respond(i, c, l, z):
        arg = c["arg"] + float(STEPS - 1) * c["arg_step"]
        u = u_ref[i, l, pl.ds(z, 8)]
        new_u = u - jnp.exp2(theta_b[i, l, pl.ds(8 + z, 8)] + (c["m"] * u + arg))
        return 10.0 - c["out"] * jnp.exp2(new_u)

    def inner(l, carry):
        prepare(HALO + 1 + 2 * l)
        prepare(HALO + 2 + 2 * l)
        return carry

    lax.fori_loop(0, (XS - 2) // 2, inner, 0)

    def ahead(i, carry):
        c = coefficients_of(loc, i)
        for n in range(STEPS - 1):
            main_step(i, c, n, HALO + 1 + n, HALO + XS - 2 - n)
        for index, when in enumerate(HAND):

            @pl.when(i == when)
            def _(index=index):
                halo[index].wait_recv()
                handed[index].start()

        return carry

    lax.fori_loop(0, MINE, ahead, 0)
    for copy in halo:
        copy.wait_send()
    for copy in handed:
        copy.wait()

    @pl.when(s_index == 0)
    def _():
        t0[HALO - 1] = jnp.zeros((ROWS + 16, 128), jnp.float32)

    @pl.when(s_index == s_count - 1)
    def _():
        t0[HALO + XS] = jnp.zeros((ROWS + 16, 128), jnp.float32)

    def outer(l, carry):
        prepare(1 + l)
        prepare(HALO + XS - 1 + l)
        return carry

    lax.fori_loop(0, HALO, outer, 0)

    def sends(i, index):
        along, across = TARGETS[index]
        target = 2 * ((y + along) % 4) + (core + across) % 2
        return pltpu.make_async_remote_copy(
            src_ref=rsp.at[i, pl.ds(pl.multiple_of(64 * target, 8), 64)],
            dst_ref=recv.at[loc * MINE + i],
            send_sem=send_sem.at[i, index],
            recv_sem=recv_sem.at[i, index],
            device_id=(zh * PEERS + target, s_index),
            device_id_type=MESH,
        )


    def rest(i, carry):
        c = coefficients_of(loc, i)
        for n in range(STEPS - 1):
            main_step(i, c, n, 1 + n, HALO + n)
            main_step(i, c, n, HALO + XS - 1 - n, LAYERS - 2 - n)
        for x in range(XS):
            for k in range(4):
                rsp[i, pl.ds(8 * k * XS + x, 8, stride=XS), :] = respond(
                    i, c, HALO + x, zero_row + 8 * k
                )
        for index in range(FAR):
            sends(i, index).start()

        @pl.when(i < MINE - TWICE)
        def _():
            for index in range(FAR, PEERS - 1):
                sends(i, index).start()

        recv[loc * MINE + i] = rsp[i, pl.ds(pl.multiple_of(64 * loc, 8), 64), :]
        return carry

    lax.fori_loop(0, MINE, rest, 0)

    partner = 2 * ((y + 2) % 4) + core
    place = zh + y
    own_row = pl.multiple_of(8 * place, 8)
    window = pl.multiple_of(8 * (place - (place + 3) // 4 - place // 4), 8)

    def hands(e):
        return pltpu.make_async_remote_copy(
            src_ref=extra.at[e, pl.ds(pl.multiple_of(64 * (1 - core), 8), 64)],
            dst_ref=recv.at[partner * MINE + MINE - TWICE + e],
            send_sem=extra_send.at[e],
            recv_sem=extra_recv.at[e],
            device_id=(sibling, s_index),
            device_id_type=MESH,
        )


    def again(e, carry):
        i = MINE - TWICE + e
        c = coefficients_of(partner, i)
        for n in range(STEPS - 2):
            step(e, c, n, 1 + n, LAYERS - 2 - n, window, 3)
        n = STEPS - 2
        step(e, c, n, 1 + n, LAYERS - 2 - n, own_row, 1, place == 0, place == 4)
        for x in range(XS):
            extra[e, pl.ds(x, 8, stride=XS), :] = respond(e, c, HALO + x, own_row)
        hands(e).start()
        recv[partner * MINE + i] = extra[e, pl.ds(pl.multiple_of(64 * core, 8), 64), :]
        return carry

    lax.fori_loop(0, TWICE, again, 0)

    def drain(i, carry):
        for index in range(FAR):
            sends(i, index).wait()

        @pl.when(i < MINE - TWICE)
        def _():
            for index in range(FAR, PEERS - 1):
                sends(i, index).wait()

        return carry

    lax.fori_loop(0, MINE, drain, 0)

    def drain_hands(e, carry):
        hands(e).wait()
        return carry

    lax.fori_loop(0, TWICE, drain_hands, 0)

    def maps(tile, carry):
        at = pl.ds(pl.multiple_of(8 * tile, 8), 8)
        resp_a = [recv[s, at, :] for s in range(SAMPLES)]
        resp_b = [recv[SAMPLES + s, at, :] for s in range(SAMPLES)]
        pooled = resp_a + resp_b
        average = sum(pooled[1:], pooled[0]) * (1.0 / len(pooled))
        spread = [(r - average) * (r - average) for r in pooled]
        variance = sum(spread[1:], spread[0]) * (1.0 / len(pooled))
        var_ref[at, :] = variance
        for g in range(GROUPS - 2):
            first = total = None
            for s in range(SAMPLES):
                mixed = recv[(g + 2) * SAMPLES + s, at, :]
                to_b, to_a = resp_b[s] - mixed, resp_a[s] - mixed
                first = to_b * to_b if first is None else first + to_b * to_b
                total = to_a * to_a if total is None else total + to_a * to_a
            first_ref[g, at, :] = variance - (0.5 / SAMPLES) * first
            total_ref[g, at, :] = (0.5 / SAMPLES) * total
        return carry

    lax.fori_loop(0, 8, maps, 0)


TARGETS = ((1, 0), (3, 0), (1, 1), (3, 1), (0, 1), (2, 0), (2, 1))
FAR = 5
TWICE = 4
HAND = (3, 5, 6)


def local(initial_density, initial_thermal, boundary_mask, samples_a, samples_b, design_index):
    vmem = pl.BlockSpec(memory_space=pltpu.VMEM)
    hbm = pl.BlockSpec(memory_space=pl.ANY)
    dma = pltpu.SemaphoreType.DMA

    def state(*shape):
        return pltpu.VMEM(shape + (128,), jnp.float32)

    first, total, variance = pl.pallas_call(
        kernel,
        out_shape=(
            jax.ShapeDtypeStruct((GROUPS - 2, 64, 128), jnp.float32),
            jax.ShapeDtypeStruct((GROUPS - 2, 64, 128), jnp.float32),
            jax.ShapeDtypeStruct((64, 128), jnp.float32),
        ),
        in_specs=[hbm] * 6,
        out_specs=(vmem, vmem, vmem),
        scratch_shapes=[
            state(ROWS * XS),
            state(ROWS * XS),
            pltpu.VMEM((ROWS * XS, 128), jnp.int32),
            pltpu.SMEM((SAMPLES, P_SIZE), jnp.float32),
            pltpu.SMEM((SAMPLES, P_SIZE), jnp.float32),
            pltpu.SMEM((P_SIZE,), jnp.int32),
            state(LAYERS, ROWS + 16),
        ]
        + [state(LAYERS, ROWS)] * 7
        + [state(MINE, LAYERS, ROWS + 16)] * 2
        + [state(MINE, LAYERS, ROWS)] * 3
        + [
            state(MINE, 512),
            state(TWICE, 128),
            state(GROUPS * SAMPLES, 64),
            dma((6,)),
            dma((3,)),
            dma((3,)),
            dma((3,)),
            dma((3,)),
            dma((MINE, PEERS - 1)),
            dma((MINE, PEERS - 1)),
            dma((TWICE,)),
            dma((TWICE,)),
        ],
        compiler_params=pltpu.CompilerParams(
            collective_id=0, has_side_effects=True, vmem_limit_bytes=54067 * 1024
        ),
    )(
        initial_density.reshape(1024, 128),
        initial_thermal.reshape(1024, 128),
        boundary_mask.reshape(1024, 128),
        samples_a,
        samples_b,
        design_index,
    )
    return (
        first.reshape(GROUPS - 2, 4, 16, 128),
        total.reshape(GROUPS - 2, 4, 16, 128),
        variance.reshape(4, 16, 128),
    )


def solution(mesh):
    return jax.shard_map(
        local,
        mesh=mesh,
        in_specs=(
            P(None, "space", None),
            P(None, "space", None),
            P(None, "space", None),
            P(),
            P(),
            P(),
        ),
        out_specs=(
            P(None, "design", "space", None),
            P(None, "design", "space", None),
            P("design", "space", None),
        ),
        check_vma=False,
    )
```
